32 devices in a mesh: gx: 2 (over core), gy: 4 (over z), gz: 4 (over y, x).
Axes of the slice: x: 2, y: 2, z: 4, core: 2. Of those that a mesh axis runs over, the one named last changes fastest.
Arguments:
- residual: float32 [32, 64, 1024], P('gx', 'gy', 'gz'), may hold values from -6 to 6
- fdm_vectors: bfloat16 [2, 4, 4, 3, 10, 10, 128], P('gx', 'gy', 'gz'), may hold values from -2 to 2
- fdm_eigen: float32 [2, 4, 4, 3, 10, 128], P('gx', 'gy', 'gz'), may hold values from 0.1 to 4
- coarse_basis: float32 [8, 8, 8], replicated, may hold values from -0.75 to 0.75
- x_interior: float32 [2, 4, 4, 16, 16], P('gx', 'gy', 'gz'), may hold values from -1.5 to 1.5
- x_separator: float32 [2, 4, 4, 5, 16, 256], P('gx', 'gy', 'gz'), may hold values from -0.375 to 0.375
Outputs:
- preconditioned: float32 [32, 64, 1024], P('gx', 'gy', 'gz')
The draws below stay inside these ranges and needn't reach their ends.
All inputs are finite; a program needn't handle non-finite values.
Results may differ from the reference program's by a relative error of at most 0.0003.
Values sent between devices are 32-bit elements; how exact they have to be, the bound alone decides.
A program may use at most 128 MiB of HBM per device.

```python
import math
import jax
import jax.numpy as jnp
from jax import lax

PTS = 8
EXT = 10
EX = 2
EY = 2
EZ = 32
KSEP = 256
ELEMS = 128
VCO = 16
CX = 16
CY = 16
CZ = 256
NX = 32
NY = 64
NZ = 1024
LEVELS = 5
N_GX = 2
N_GY = 4
N_GZ = 4


def block_levels(rng, extent, shards, low, largest):
    def one(dim, blocks):
        steps = jax.random.uniform(jax.random.fold_in(jax.random.fold_in(rng, 6), dim), (blocks,), jnp.float32, low / len(shards), largest / len(shards))
        return jnp.repeat(jnp.exp(steps), extent[dim] // blocks).reshape((-1,) + (1,) * (len(extent) - dim - 1))

    factor_of = one(*shards[0])
    for cut in shards[1:]:
        factor_of = factor_of * one(*cut)
    return factor_of


def normal_values(rng, extent, deviation, limit, shards=(), kind=jnp.bfloat16):
    drawn = deviation * jax.random.normal(rng, extent, jnp.float32)
    if shards:
        drawn = drawn * block_levels(rng, extent, shards, -0.22, 0.18)
    return jnp.clip(drawn, -limit, limit).astype(kind)


def setup_inputs(seed: int = 0) -> dict:
    arg_keys = jax.random.split(jax.random.key(seed), 7)
    residual = normal_values(arg_keys[0], (NX, NY, NZ), 1.0, 6.0, ((0, 2), (1, 4), (2, 4)), jnp.float32)
    fdm_vectors = normal_values(arg_keys[1], (N_GX, N_GY, N_GZ, 3, EXT, EXT, ELEMS), EXT ** -0.5, 2.0, ((0, 2), (1, 4), (2, 4)))
    fdm_eigen = jnp.clip(jnp.exp(math.log(4.0) - 3.6888794 * jax.random.uniform(arg_keys[2], (N_GX, N_GY, N_GZ, 3, EXT, ELEMS), jnp.float32) ** block_levels(arg_keys[2], (N_GX, N_GY, N_GZ, 3, EXT, ELEMS), ((0, 2), (1, 4), (2, 4)), -0.2, 0.2)), 0.1, 4.0)
    coarse_basis = normal_values(arg_keys[3], (PTS, PTS, PTS), 0.125, 0.75, (), jnp.float32)
    x_interior = normal_values(arg_keys[4], (N_GX, N_GY, N_GZ, VCO, VCO), VCO ** -0.5, 1.5, ((0, 2), (1, 4), (2, 4)), jnp.float32)
    x_separator = normal_values(arg_keys[5], (N_GX, N_GY, N_GZ, LEVELS, VCO, KSEP), (VCO * 16) ** -0.5, 0.375, ((0, 2), (1, 4), (2, 4)), jnp.float32)
    return dict(residual=residual, fdm_vectors=fdm_vectors, fdm_eigen=fdm_eigen, coarse_basis=coarse_basis, x_interior=x_interior, x_separator=x_separator)


HIGHEST = lax.Precision.HIGHEST


def extend_block(padded, count_x, count_y, count_z):
    along_x = jnp.stack([lax.slice_in_dim(padded, i, i + PTS * (count_x - 1) + 1, PTS, 0) for i in range(PTS + 2)], 0)
    along_y = jnp.stack([lax.slice_in_dim(along_x, j, j + PTS * (count_y - 1) + 1, PTS, 2) for j in range(PTS + 2)], 1)
    along_z = jnp.stack([lax.slice_in_dim(along_y, k, k + PTS * (count_z - 1) + 1, PTS, 4) for k in range(PTS + 2)], 2)
    return along_z.reshape(PTS + 2, PTS + 2, PTS + 2, count_x * count_y * count_z)


def solve_elements(extended, vectors, eigen):
    modes_x = vectors[0].astype(jnp.float32)
    modes_y = vectors[1].astype(jnp.float32)
    modes_z = vectors[2].astype(jnp.float32)
    temp = jnp.einsum('iae,ijke->ajke', modes_x, extended, precision=HIGHEST)
    temp = jnp.einsum('jbe,ajke->abke', modes_y, temp, precision=HIGHEST)
    temp = jnp.einsum('kce,abke->abce', modes_z, temp, precision=HIGHEST)
    denom = eigen[0][:, None, None, :] + eigen[1][None, :, None, :] + eigen[2][None, None, :, :]
    temp = temp / denom
    temp = jnp.einsum('iae,abce->ibce', modes_x, temp, precision=HIGHEST)
    temp = jnp.einsum('jbe,ibce->ijce', modes_y, temp, precision=HIGHEST)
    temp = jnp.einsum('kce,ijce->ijke', modes_z, temp, precision=HIGHEST)
    return temp


def fold_block(local, count_x, count_y, count_z, shape):
    grid = local.reshape(PTS + 2, PTS + 2, PTS + 2, count_x, count_y, count_z)
    filler = jnp.float32(0)
    summed_z = None
    for k in range(PTS + 2):
        config = ((0, 0, 0), (0, 0, 0), (0, 0, 0), (0, 0, 0), (k, shape[2] - k - PTS * (count_z - 1) - 1, PTS - 1))
        placed = lax.pad(grid[:, :, k], filler, config)
        summed_z = placed if summed_z is None else summed_z + placed
    summed_y = None
    for j in range(PTS + 2):
        config = ((0, 0, 0), (0, 0, 0), (j, shape[1] - j - PTS * (count_y - 1) - 1, PTS - 1), (0, 0, 0))
        placed = lax.pad(summed_z[:, j], filler, config)
        summed_y = placed if summed_y is None else summed_y + placed
    summed_x = None
    for i in range(PTS + 2):
        config = ((i, shape[0] - i - PTS * (count_x - 1) - 1, PTS - 1), (0, 0, 0), (0, 0, 0))
        placed = lax.pad(summed_y[i], filler, config)
        summed_x = placed if summed_x is None else summed_x + placed
    return summed_x


def schwarz_block(padded, vectors, eigen):
    extended = extend_block(padded, EX, EY, EZ)
    local = solve_elements(extended, vectors, eigen)
    return fold_block(local, EX, EY, EZ, padded.shape)


def reference(residual, fdm_vectors, fdm_eigen, coarse_basis, x_interior, x_separator):
    devices = N_GX * N_GY * N_GZ
    padded = jnp.pad(residual, 1)
    vectors_all = fdm_vectors.reshape(devices, 3, PTS + 2, PTS + 2, EX * EY * EZ)
    eigen_all = fdm_eigen.reshape(devices, 3, PTS + 2, EX * EY * EZ)

    def visit(accum, item):
        number, vectors, eigen = item
        start_x = (number // (N_GY * N_GZ)) * CX
        start_y = ((number // N_GZ) % N_GY) * CY
        start_z = (number % N_GZ) * CZ
        starts = (start_x.astype(jnp.int32), start_y.astype(jnp.int32), start_z.astype(jnp.int32))
        sizes = (CX + 2, CY + 2, CZ + 2)
        block = lax.dynamic_slice(padded, starts, sizes)
        contrib = schwarz_block(block, vectors, eigen)
        current = lax.dynamic_slice(accum, starts, sizes)
        return lax.dynamic_update_slice(accum, current + contrib, starts), None

    numbers = jnp.arange(devices, dtype=jnp.int32)
    accum, _ = lax.scan(visit, jnp.zeros_like(padded), (numbers, vectors_all, eigen_all))
    smoothed = accum[1:-1, 1:-1, 1:-1]

    view = (NX // (2 * PTS), 2, PTS, NY // (2 * PTS), 2, PTS, NZ // (2 * PTS), 2, PTS)
    weights = coarse_basis[None, None, :, None, None, :, None, None, :]
    rhs_grid = jnp.sum(residual.reshape(view) * weights, axis=(1, 2, 4, 5, 7, 8))
    coarse_rhs = rhs_grid.reshape(N_GX, EX // 2, N_GY, EY // 2, N_GZ, EZ // 2)
    coarse_rhs = coarse_rhs.transpose(0, 2, 4, 1, 3, 5).reshape(devices, VCO)

    own = x_interior.reshape(devices, VCO, VCO)
    seps = x_separator.reshape(devices, LEVELS, VCO, KSEP)
    interior_coef = jnp.einsum('dvw,dv->dw', own, coarse_rhs, precision=HIGHEST)
    partials = jnp.einsum('dlvk,dv->dlk', seps, coarse_rhs, precision=HIGHEST)
    groups = []
    for level in range(1, LEVELS + 1):
        width = 2 ** level
        summed = partials[:, level - 1].reshape(devices // width, width, KSEP).sum(axis=1)
        groups.append(jnp.repeat(summed, width, axis=0))
    separator_coef = jnp.stack(groups, 1)
    coarse_solution = jnp.einsum('dvw,dw->dv', own, interior_coef, precision=HIGHEST)
    coarse_solution = coarse_solution + jnp.einsum('dlvk,dlk->dv', seps, separator_coef, precision=HIGHEST)

    coarse_grid = coarse_solution.reshape(N_GX, N_GY, N_GZ, EX // 2, EY // 2, EZ // 2)
    coarse_grid = coarse_grid.transpose(0, 3, 1, 4, 2, 5).reshape(NX // (2 * PTS), NY // (2 * PTS), NZ // (2 * PTS))
    correction = coarse_grid[:, None, None, :, None, None, :, None, None] * weights
    preconditioned = smoothed.reshape(view) + correction
    return preconditioned.reshape(NX, NY, NZ)
```

```python
import functools

import jax
import jax.numpy as jnp
import numpy as np
from jax import lax
from jax.experimental import pallas as pl
from jax.experimental.pallas import tpu as pltpu
from jax.sharding import PartitionSpec as P

PTS = 8
EXT = PTS + 2
ROWS = 16
HIGHEST = lax.Precision.HIGHEST
F32 = jnp.float32
BF16 = jnp.bfloat16


def selection(groups, count):
    lanes = groups * count
    size = count * PTS
    matrix = np.zeros((groups * size + 128, EXT * lanes), np.float32)
    for g in range(groups):
        for r in range(count):
            for k in range(EXT):
                z = PTS * r + k - 1
                row = g * size + z
                if z < 0:
                    row = groups * size + 2 * g
                elif z >= size:
                    row = groups * size + 2 * g + 1
                matrix[row, k * lanes + g * count + r] = 1
    return matrix


def halves(value):
    high = value.astype(BF16)
    return high, (value - high.astype(F32)).astype(BF16)


def prepare_modes(vec_ref, eig_ref, modes, lam, lamx):
    def spread(n, _):
        d, i = n // EXT, n % EXT
        rows = vec_ref[d, i].astype(F32)
        for a in range(EXT):
            modes[pl.ds(pl.multiple_of((n * EXT + a) * 8, 8), 8), :] = jnp.broadcast_to(rows[a : a + 1], (8, 128))
        return 0

    lax.fori_loop(0, 3 * EXT, spread, 0)
    for d in range(2):
        rows = eig_ref[d + 1]
        for a in range(EXT):
            lam[(d * EXT + a) * 8 : (d * EXT + a + 1) * 8, :] = jnp.broadcast_to(rows[a : a + 1], (8, 128))
    lamx[...] = jnp.ones_like(lamx)
    lamx[0:EXT, :] = eig_ref[0]


def gather_elements(grid_ref, ends_ref, sel_ref, parts, buf, ex, ey):
    groups = ex * ey
    size = grid_ref.shape[2]
    rows = EXT * ROWS
    ends = None
    for g in range(groups):
        x, y = PTS * (g // ey), PTS * (g % ey)
        block = grid_ref[x : x + EXT, y : y + ROWS, :].reshape(rows, size)
        high, low = halves(block)
        parts[0:rows, g * size : (g + 1) * size] = high
        parts[rows : 2 * rows, g * size : (g + 1) * size] = low
        side = ends_ref[x : x + EXT, y : y + ROWS, :].reshape(rows, 128)
        side = side if g == 0 else pltpu.roll(side, 2 * g, 1)
        ends = side if ends is None else ends + side
    high, low = halves(ends)
    width = groups * size
    parts[0:rows, width : width + 128] = high
    parts[rows : 2 * rows, width : width + 128] = low
    for pair in range(EXT // 2):
        columns = slice(pair * 256, (pair + 1) * 256)
        both = jnp.dot(parts[:, 0:width], sel_ref[0:width, columns], preferred_element_type=F32)
        if pair in (0, EXT // 2 - 1):
            both = both + jnp.dot(
                parts[:, width : width + 128], sel_ref[width : width + 128, columns], preferred_element_type=F32
            )
        total = both[0:rows] + both[rows : 2 * rows]
        buf[2 * pair * rows : (2 * pair + 1) * rows, :] = total[:, 0:128]
        buf[(2 * pair + 1) * rows : (2 * pair + 2) * rows, :] = total[:, 128:256]


def contract(values, modes, d, back):
    out = []
    for p in range(EXT):
        total = None
        for q in range(EXT):
            i, a = (p, q) if back else (q, p)
            start = ((d * EXT + i) * EXT + a) * 8
            term = modes[start : start + 8, :][None] * values[q]
            total = term if total is None else total + term
        out.append(total)
    return out


def tile(ref, start):
    return ref[pl.ds(start, ROWS), :].reshape(2, 8, 128)


def put(ref, start, value):
    ref[pl.ds(start, ROWS), :] = value.reshape(ROWS, 128)


def along_z(buf, modes, back):
    def body(i, _):
        at = [pl.multiple_of((k * EXT + i) * ROWS, ROWS) for k in range(EXT)]
        out = contract([tile(buf, s) for s in at], modes, 2, back)
        for s, value in zip(at, out):
            put(buf, s, value)
        return 0

    lax.fori_loop(0, EXT, body, 0)


def along_xy(buf, turn, modes, lam, lamx):
    def body(c, _):
        at = [pl.multiple_of((c * EXT + i) * ROWS, ROWS) for i in range(EXT)]
        t = contract([tile(buf, s) for s in at], modes, 0, False)
        for a in range(EXT):
            turn[a * ROWS : (a + 1) * ROWS, :] = t[a].reshape(ROWS, 128)
        t = [turn[pl.ds(j, ROWS, ROWS), :].reshape(2, 8, 128) for j in range(EXT)]
        t = contract(t, modes, 1, False)
        first = lamx[...].reshape(2, 8, 128)
        third = lam[pl.ds(pl.multiple_of((EXT + c) * 8, 8), 8), :][None]
        t = [v / (first + lam[b * 8 : (b + 1) * 8, :][None] + third) for b, v in enumerate(t)]
        t = contract(t, modes, 1, True)
        for j in range(EXT):
            turn[j * ROWS : (j + 1) * ROWS, :] = t[j].reshape(ROWS, 128)
        t = [turn[pl.ds(a, ROWS, ROWS), :].reshape(2, 8, 128) for a in range(EXT)]
        t = contract(t, modes, 0, True)
        for s, value in zip(at, t):
            put(buf, s, value)
        return 0

    lax.fori_loop(0, EXT, body, 0)


def scatter_elements(buf, sel_ref, parts, grid_ref, ends_ref, ex, ey):
    groups = ex * ey
    size = grid_ref.shape[2]
    rows = EXT * ROWS
    lanes = EXT * 128
    for k in range(EXT):
        high, low = halves(buf[k * rows : (k + 1) * rows, :])
        parts[0:rows, k * 128 : (k + 1) * 128] = high
        parts[rows : 2 * rows, k * 128 : (k + 1) * 128] = low
    dims = (((1,), (1,)), ((), ()))
    grid_ref[...] = jnp.zeros_like(grid_ref)
    ends_ref[...] = jnp.zeros_like(ends_ref)
    width = groups * size
    both = lax.dot_general(
        parts[:, 0:lanes], sel_ref[width : width + 128, :], dims, preferred_element_type=F32
    )
    ends = both[0:rows] + both[rows : 2 * rows]
    lane = lax.broadcasted_iota(jnp.int32, (1, 128), 1)
    for g in range(groups):
        x, y = PTS * (g // ey), PTS * (g % ey)
        both = lax.dot_general(
            parts[:, 0:lanes], sel_ref[g * size : (g + 1) * size, :], dims, preferred_element_type=F32
        )
        total = (both[0:rows] + both[rows : 2 * rows]).reshape(EXT, ROWS, size)
        grid_ref[x : x + EXT, y : y + EXT, :] += total[:, 0:EXT]
        side = ends if g == 0 else pltpu.roll(ends, 128 - 2 * g, 1)
        side = jnp.where(lane < 2, side, 0.0).reshape(EXT, ROWS, 128)
        ends_ref[x : x + EXT, y : y + EXT, :] += side[:, 0:EXT]


def smooth_kernel(ex, ey, grid_in, ends_in, vec, eig, sel, grid_out, ends_out, parts, buf, turn, modes, lam, lamx):
    turn[...] = jnp.zeros_like(turn)
    prepare_modes(vec, eig, modes, lam, lamx)
    gather_elements(grid_in, ends_in, sel, parts, buf, ex, ey)
    along_z(buf, modes, False)
    along_xy(buf, turn, modes, lam, lamx)
    along_z(buf, modes, True)
    scatter_elements(buf, sel, parts, grid_out, ends_out, ex, ey)


def smooth_call(padded, vectors, eigen, ex, ey, ez):
    nx, ny, nz = padded.shape
    size = nz - 2
    tall = PTS * (ey - 1) + ROWS
    sel = jnp.asarray(selection(ex * ey, ez), BF16)
    grid = jnp.pad(padded[:, :, 1:-1], ((0, 0), (0, tall - ny), (0, 0)))
    ends = jnp.stack([padded[:, :, 0], padded[:, :, -1]], -1)
    ends = jnp.pad(ends, ((0, 0), (0, tall - ny), (0, 126)))
    vmem = pl.BlockSpec(memory_space=pltpu.VMEM)
    rows = EXT * ROWS
    out, sides = pl.pallas_call(
        functools.partial(smooth_kernel, ex, ey),
        out_shape=(
            jax.ShapeDtypeStruct((nx, tall, size), F32),
            jax.ShapeDtypeStruct((nx, tall, 128), F32),
        ),
        in_specs=[vmem] * 5,
        out_specs=(vmem, vmem),
        scratch_shapes=[
            pltpu.VMEM((2 * rows, max(sel.shape)), BF16),
            pltpu.VMEM((EXT * rows, 128), F32),
            pltpu.VMEM((ROWS * ROWS, 128), F32),
            pltpu.VMEM((3 * EXT * EXT * 8, 128), F32),
            pltpu.VMEM((2 * EXT * 8, 128), F32),
            pltpu.VMEM((ROWS, 128), F32),
        ],
        compiler_params=pltpu.CompilerParams(vmem_limit_bytes=40 * 1024 * 1024),
        name="smooth",
    )(grid, ends, vectors, eigen, sel)
    return jnp.concatenate([sides[:, :ny, 0:1], out[:, :ny], sides[:, :ny, 1:2]], 2)


def extended_2(cells, sides, width):
    for axis, dim in sides:
        count = lax.axis_size(axis)
        ends = count - 1
        head = lax.slice_in_dim(cells, 0, width, axis=dim)
        tail = lax.slice_in_dim(cells, cells.shape[dim] - width, cells.shape[dim], axis=dim)
        cells = jnp.concatenate(
            [
                lax.ppermute(tail, axis, [(i, (i + 1) % count) for i in range(ends)]),
                cells,
                lax.ppermute(head, axis, [((i + 1) % count, i) for i in range(ends)]),
            ],
            axis=dim,
        )
    return cells


def swapped(array, axis, distance):
    return lax.ppermute(array, axis, [(i, i ^ 1 << distance) for i in range(lax.axis_size(axis))])


def folded_in(value, axis, dim):
    count = lax.axis_size(axis)
    size = value.shape[dim]
    low = lax.slice_in_dim(value, 0, 1, axis=dim)
    high = lax.slice_in_dim(value, size - 1, size, axis=dim)
    below = lax.ppermute(high, axis, [(i, i + 1) for i in range(count - 1)])
    above = lax.ppermute(low, axis, [(i + 1, i) for i in range(count - 1)])
    first = lax.slice_in_dim(value, 1, 2, axis=dim) + below
    last = lax.slice_in_dim(value, size - 2, size - 1, axis=dim) + above
    return jnp.concatenate([first, lax.slice_in_dim(value, 2, size - 2, axis=dim), last], dim)


def on_device(residual, fdm_vectors, fdm_eigen, coarse_basis, x_interior, x_separator):
    cx, cy, cz = residual.shape
    ex, ey, ez = cx // PTS, cy // PTS, cz // PTS
    padded = extended_2(residual, (("gx", 0), ("gy", 1), ("gz", 2)), 1)
    vectors = fdm_vectors.reshape(fdm_vectors.shape[3:])
    eigen = fdm_eigen.reshape(fdm_eigen.shape[3:])
    folded = smooth_call(padded, vectors, eigen, ex, ey, ez)
    for dim, axis in enumerate(("gx", "gy", "gz")):
        folded = folded_in(folded, axis, dim)

    view = (ex // 2, 2, PTS, ey // 2, 2, PTS, ez // 2, 2, PTS)
    weights = coarse_basis[None, None, :, None, None, :, None, None, :]
    coarse_rhs = jnp.sum(residual.reshape(view) * weights, axis=(1, 2, 4, 5, 7, 8)).reshape(-1)
    unknowns = coarse_rhs.shape[0]
    own_factor = x_interior.reshape(unknowns, unknowns)
    levels = x_separator.shape[3]
    sep_factor = x_separator.reshape(levels, unknowns, x_separator.shape[5])
    interior_coef = jnp.dot(coarse_rhs, own_factor, precision=HIGHEST)
    running = jnp.einsum("lvk,v->lk", sep_factor, coarse_rhs, precision=HIGHEST)
    finished = 0
    for axis in ("gz", "gy", "gx"):
        for b in range(lax.axis_size(axis).bit_length() - 1):
            pending = running[finished:]
            running = jnp.concatenate([running[:finished], pending + swapped(pending, axis, b)], 0)
            finished = finished + 1
    coarse_solution = jnp.dot(own_factor, interior_coef, precision=HIGHEST)
    coarse_solution = coarse_solution + jnp.einsum("lvk,lk->v", sep_factor, running, precision=HIGHEST)
    cells = coarse_solution.reshape(ex // 2, 1, 1, ey // 2, 1, 1, ez // 2, 1, 1)
    correction = jnp.broadcast_to(cells * weights, view).reshape(cx, cy, cz)
    return folded + correction


def solution(mesh):
    in_specs = (
        P("gx", "gy", "gz"),
        P("gx", "gy", "gz", None, None, None, None),
        P("gx", "gy", "gz", None, None, None),
        P(),
        P("gx", "gy", "gz", None, None),
        P("gx", "gy", "gz", None, None, None),
    )
    out_specs = P("gx", "gy", "gz")
    return jax.shard_map(
        on_device, mesh=mesh, in_specs=in_specs, out_specs=out_specs, check_vma=False
    )
```

```python
import functools

import jax
import jax.numpy as jnp
import numpy as np
from jax import lax
from jax.experimental import pallas as pl
from jax.experimental.pallas import tpu as pltpu
from jax.sharding import PartitionSpec as P

PTS = 8
EXT = PTS + 2
ROWS = 16
F32 = jnp.float32
BF16 = jnp.bfloat16


def selection(groups, count):
    lanes = groups * count
    size = count * PTS
    matrix = np.zeros((groups * size + 128, EXT * lanes), np.float32)
    for g in range(groups):
        for r in range(count):
            for k in range(EXT):
                z = PTS * r + k - 1
                row = g * size + z
                if z < 0:
                    row = groups * size + 2 * g
                elif z >= size:
                    row = groups * size + 2 * g + 1
                matrix[row, k * lanes + g * count + r] = 1
    return matrix


def halves(value):
    high = value.astype(BF16)
    return high, (value - high.astype(F32)).astype(BF16)


def prepare_modes(vec_ref, eig_ref, modes, lam, lamx):
    def spread(n, _):
        d, i = n // EXT, n % EXT
        rows = vec_ref[d, i].astype(F32)
        for a in range(EXT):
            modes[pl.ds(pl.multiple_of((n * EXT + a) * 8, 8), 8), :] = jnp.broadcast_to(rows[a : a + 1], (8, 128))
        return 0

    lax.fori_loop(0, 3 * EXT, spread, 0)
    for d in range(2):
        rows = eig_ref[d + 1]
        for a in range(EXT):
            lam[(d * EXT + a) * 8 : (d * EXT + a + 1) * 8, :] = jnp.broadcast_to(rows[a : a + 1], (8, 128))
    lamx[...] = jnp.ones_like(lamx)
    lamx[0:EXT, :] = eig_ref[0]


def gather_elements(grid_ref, ends_ref, sel_ref, parts, buf, ex, ey):
    groups = ex * ey
    size = grid_ref.shape[2]
    rows = EXT * ROWS
    ends = None
    for g in range(groups):
        x, y = PTS * (g // ey), PTS * (g % ey)
        block = grid_ref[x : x + EXT, y : y + ROWS, :].reshape(rows, size)
        high, low = halves(block)
        parts[0:rows, g * size : (g + 1) * size] = high
        parts[rows : 2 * rows, g * size : (g + 1) * size] = low
        side = ends_ref[x : x + EXT, y : y + ROWS, :].reshape(rows, 128)
        side = side if g == 0 else pltpu.roll(side, 2 * g, 1)
        ends = side if ends is None else ends + side
    high, low = halves(ends)
    width = groups * size
    parts[0:rows, width : width + 128] = high
    parts[rows : 2 * rows, width : width + 128] = low
    for pair in range(EXT // 2):
        columns = slice(pair * 256, (pair + 1) * 256)
        both = jnp.dot(parts[:, 0:width], sel_ref[0:width, columns], preferred_element_type=F32)
        if pair in (0, EXT // 2 - 1):
            both = both + jnp.dot(
                parts[:, width : width + 128], sel_ref[width : width + 128, columns], preferred_element_type=F32
            )
        total = both[0:rows] + both[rows : 2 * rows]
        buf[2 * pair * rows : (2 * pair + 1) * rows, :] = total[:, 0:128]
        buf[(2 * pair + 1) * rows : (2 * pair + 2) * rows, :] = total[:, 128:256]


def contract(values, modes, d, back):
    out = []
    for p in range(EXT):
        total = None
        for q in range(EXT):
            i, a = (p, q) if back else (q, p)
            start = ((d * EXT + i) * EXT + a) * 8
            term = modes[start : start + 8, :][None] * values[q]
            total = term if total is None else total + term
        out.append(total)
    return out


def tile(ref, start):
    return ref[pl.ds(start, ROWS), :].reshape(2, 8, 128)


def put(ref, start, value):
    ref[pl.ds(start, ROWS), :] = value.reshape(ROWS, 128)


def along_z(buf, modes, back):
    def body(i, _):
        at = [pl.multiple_of((k * EXT + i) * ROWS, ROWS) for k in range(EXT)]
        out = contract([tile(buf, s) for s in at], modes, 2, back)
        for s, value in zip(at, out):
            put(buf, s, value)
        return 0

    lax.fori_loop(0, EXT, body, 0)


def along_xy(buf, turn, modes, lam, lamx):
    def body(c, _):
        at = [pl.multiple_of((c * EXT + i) * ROWS, ROWS) for i in range(EXT)]
        t = contract([tile(buf, s) for s in at], modes, 0, False)
        for a in range(EXT):
            turn[a * ROWS : (a + 1) * ROWS, :] = t[a].reshape(ROWS, 128)
        t = [turn[pl.ds(j, ROWS, ROWS), :].reshape(2, 8, 128) for j in range(EXT)]
        t = contract(t, modes, 1, False)
        first = lamx[...].reshape(2, 8, 128)
        third = lam[pl.ds(pl.multiple_of((EXT + c) * 8, 8), 8), :][None]
        t = [v / (first + lam[b * 8 : (b + 1) * 8, :][None] + third) for b, v in enumerate(t)]
        t = contract(t, modes, 1, True)
        for j in range(EXT):
            turn[j * ROWS : (j + 1) * ROWS, :] = t[j].reshape(ROWS, 128)
        t = [turn[pl.ds(a, ROWS, ROWS), :].reshape(2, 8, 128) for a in range(EXT)]
        t = contract(t, modes, 0, True)
        for s, value in zip(at, t):
            put(buf, s, value)
        return 0

    lax.fori_loop(0, EXT, body, 0)


def scatter_elements(buf, sel_ref, parts, grid_ref, ends_ref, ex, ey):
    groups = ex * ey
    size = grid_ref.shape[2]
    rows = EXT * ROWS
    lanes = EXT * 128
    for k in range(EXT):
        high, low = halves(buf[k * rows : (k + 1) * rows, :])
        parts[0:rows, k * 128 : (k + 1) * 128] = high
        parts[rows : 2 * rows, k * 128 : (k + 1) * 128] = low
    dims = (((1,), (1,)), ((), ()))
    grid_ref[...] = jnp.zeros_like(grid_ref)
    ends_ref[...] = jnp.zeros_like(ends_ref)
    width = groups * size
    both = lax.dot_general(
        parts[:, 0:lanes], sel_ref[width : width + 128, :], dims, preferred_element_type=F32
    )
    ends = both[0:rows] + both[rows : 2 * rows]
    lane = lax.broadcasted_iota(jnp.int32, (1, 128), 1)
    for g in range(groups):
        x, y = PTS * (g // ey), PTS * (g % ey)
        both = lax.dot_general(
            parts[:, 0:lanes], sel_ref[g * size : (g + 1) * size, :], dims, preferred_element_type=F32
        )
        total = (both[0:rows] + both[rows : 2 * rows]).reshape(EXT, ROWS, size)
        grid_ref[x : x + EXT, y : y + EXT, :] += total[:, 0:EXT]
        side = ends if g == 0 else pltpu.roll(ends, 128 - 2 * g, 1)
        side = jnp.where(lane < 2, side, 0.0).reshape(EXT, ROWS, 128)
        ends_ref[x : x + EXT, y : y + EXT, :] += side[:, 0:EXT]


def smooth_kernel(ex, ey, grid_in, ends_in, vec, eig, sel, out, parts, buf, turn, modes, lam, lamx):
    size = grid_in.shape[2]
    grid_out, ends_out = out.at[:, :, 0:size], out.at[:, :, size : size + 128]
    turn[...] = jnp.zeros_like(turn)
    prepare_modes(vec, eig, modes, lam, lamx)
    gather_elements(grid_in, ends_in, sel, parts, buf, ex, ey)
    along_z(buf, modes, False)
    along_xy(buf, turn, modes, lam, lamx)
    along_z(buf, modes, True)
    scatter_elements(buf, sel, parts, grid_out, ends_out, ex, ey)


def smooth_call(grid, ends, vectors, eigen, ex, ey, ez):
    nx, tall, size = grid.shape
    sel = jnp.asarray(selection(ex * ey, ez), BF16)
    vmem = pl.BlockSpec(memory_space=pltpu.VMEM)
    rows = EXT * ROWS
    return pl.pallas_call(
        functools.partial(smooth_kernel, ex, ey),
        out_shape=jax.ShapeDtypeStruct((nx, tall, size + 128), F32),
        in_specs=[vmem] * 5,
        out_specs=vmem,
        scratch_shapes=[
            pltpu.VMEM((2 * rows, max(sel.shape)), BF16),
            pltpu.VMEM((EXT * rows, 128), F32),
            pltpu.VMEM((ROWS * ROWS, 128), F32),
            pltpu.VMEM((3 * EXT * EXT * 8, 128), F32),
            pltpu.VMEM((2 * EXT * 8, 128), F32),
            pltpu.VMEM((ROWS, 128), F32),
        ],
        compiler_params=pltpu.CompilerParams(vmem_limit_bytes=40 * 1024 * 1024),
        name="smooth",
    )(grid, ends, vectors, eigen, sel)


AXES = ("gx", "gy", "gz")
MESH = pl.DeviceIdType.MESH


def tree_bits(sizes):
    return [(a, 1 << b) for a in (2, 1, 0) for b in range(sizes[a].bit_length() - 1)]


def greet(sizes, here, bits):
    barrier = pltpu.get_barrier_semaphore()
    for a in range(3):
        for step in (-1, 1):
            @pl.when((here[a] + step >= 0) & (here[a] + step < sizes[a]))
            def _(a=a, step=step):
                pl.semaphore_signal(barrier, inc=1, device_id={AXES[a]: here[a] + step}, device_id_type=MESH)
    for a, bit in bits:
        pl.semaphore_signal(barrier, inc=1, device_id={AXES[a]: partner(here[a], bit)}, device_id_type=MESH)
    peers = len(bits)
    for a in range(3):
        peers = peers + jnp.where(here[a] > 0, 1, 0) + jnp.where(here[a] < sizes[a] - 1, 1, 0)
    pl.semaphore_wait(barrier, peers)


def partner(index, bit):
    return index + bit * (1 - 2 * ((index // bit) % 2))


class Sides:
    def __init__(self, a, sizes, here, low, high, slots, sent, came):
        self.below, self.above = here[a] > 0, here[a] < sizes[a] - 1
        self.down = pltpu.make_async_remote_copy(
            low, slots.at[1], sent.at[2 * a], came.at[2 * a + 1],
            device_id={AXES[a]: here[a] - 1}, device_id_type=MESH,
        )
        self.up = pltpu.make_async_remote_copy(
            high, slots.at[0], sent.at[2 * a + 1], came.at[2 * a],
            device_id={AXES[a]: here[a] + 1}, device_id_type=MESH,
        )

    def start(self):
        pl.when(self.below)(self.down.start)
        pl.when(self.above)(self.up.start)

    def arrive(self):
        pl.when(self.below)(self.up.wait_recv)
        pl.when(self.above)(self.down.wait_recv)

    def finish(self):
        pl.when(self.below)(self.down.wait_send)
        pl.when(self.above)(self.up.wait_send)


class Tree:
    def __init__(self, bits, first, here, slots, inbox, sent, came):
        self.first, self.slots, self.inbox = first, slots, inbox
        self.copies = [
            pltpu.make_async_remote_copy(
                slots.at[n], inbox.at[n], sent.at[n], came.at[n],
                device_id={AXES[a]: partner(here[a], bit)}, device_id_type=MESH,
            )
            for n, (a, bit) in enumerate(bits)
        ]

    def start(self, n):
        if n < len(self.copies):
            self.copies[n].start()

    def step(self, n):
        if n < len(self.copies):
            self.copies[n].wait_recv()
            level = lax.broadcasted_iota(jnp.int32, self.slots.shape[1:], 0)
            self.slots[n + 1] = self.slots[n] + jnp.where(level >= self.first + n, self.inbox[n], 0.0)

    def finish(self):
        for copy in self.copies:
            copy.wait_send()


def place():
    return [lax.axis_index(axis) for axis in AXES]


def halo_kernel(sizes, bits, res, basis, own, sep, grid, ends, run, base, xin, yout, yin, zout, zin, slots, inbox,
                sent, came, tree_sent, tree_came):
    cx, cy, size = res.shape
    nx, tall = cx + 2, grid.shape[1]
    here = place()
    for ref in (xin, yin, zin, grid, slots, yout):
        ref[...] = jnp.zeros_like(ref)
    greet(sizes, here, bits)
    along_x = Sides(0, sizes, here, res.at[0], res.at[cx - 1], xin, sent, came)
    along_x.start()

    span = 2 * PTS
    weighted = jnp.zeros((PTS, size), F32)
    for x in range(cx):
        for y in range(0, cy, PTS):
            weighted = weighted + res[x, y : y + PTS, :] * basis[x % PTS]
    unknowns = own.shape[0]
    line = jnp.sum(weighted, axis=0, keepdims=True)
    inside = lax.broadcasted_iota(jnp.int32, (unknowns, size), 1) // span == lax.broadcasted_iota(
        jnp.int32, (unknowns, size), 0
    )
    rhs = jnp.sum(jnp.where(inside, line, 0.0), axis=1, keepdims=True)
    for l in range(sep.shape[0]):
        slots[0, l : l + 1, :] = jnp.sum(sep[l] * rhs, axis=0, keepdims=True)
    tree = Tree(bits, 0, here, slots, inbox, tree_sent, tree_came)
    tree.start(0)
    coef = jnp.sum(own[...] * rhs, axis=0, keepdims=True)
    base[...] = jnp.broadcast_to(jnp.sum(own[...] * coef, axis=1, keepdims=True), base.shape)
    for x in range(cx):
        grid[x + 1, 1 : cy + 1, :] = res[x]

    along_x.arrive()
    grid[0, 1 : cy + 1, :] = xin[0]
    grid[nx - 1, 1 : cy + 1, :] = xin[1]
    for x in range(nx):
        yout[0, x : x + 1, :] = grid[x, 1:2, :]
        yout[1, x : x + 1, :] = grid[x, cy : cy + 1, :]
    along_y = Sides(1, sizes, here, yout.at[0], yout.at[1], yin, sent, came)
    along_y.start()
    tree.step(0)
    tree.start(1)
    along_y.arrive()
    for x in range(nx):
        grid[x, 0:1, :] = yin[0, x : x + 1, :]
        grid[x, cy + 1 : cy + 2, :] = yin[1, x : x + 1, :]

    lane = lax.broadcasted_iota(jnp.int32, (1, 128), 1)
    rows = nx * tall
    padded = zout.shape[2]
    flat = grid[...].reshape(rows, size)
    both = jnp.where(lane == 0, flat[:, 0:128], flat[:, size - 128 : size])
    both = jnp.concatenate([both, jnp.zeros((padded - rows, 128), F32)], 0)
    turned = both.T
    zout[0] = turned[0:8]
    zout[1] = turned[120:128]
    along_z = Sides(2, sizes, here, zout.at[0], zout.at[1], zin, sent, came)
    along_z.start()
    tree.step(1)
    tree.start(2)
    along_z.arrive()
    row = lax.broadcasted_iota(jnp.int32, (8, padded), 0)
    head = jnp.where(row == 0, zin[0, 7:8, :], jnp.where(row == 1, zin[1, 0:1, :], 0.0))
    turned = jnp.concatenate([head, jnp.zeros((120, padded), F32)], 0).T
    ends[...] = turned[0:rows].reshape(nx, tall, 128)
    for n in range(2, len(bits)):
        tree.step(n)
        tree.start(n + 1)
    run[...] = slots[len(bits)]
    for sides in (along_x, along_y, along_z):
        sides.finish()
    tree.finish()


def fold_kernel(sizes, bits, first, fold, basis, sep, run, base, out, acc, xin, yout, yin, zout, zin, slots, inbox,
                sent, came, tree_sent, tree_came):
    cx, cy, size = out.shape
    nx, tall = cx + 2, fold.shape[1]
    here = place()
    for ref in (xin, yin, zin):
        ref[...] = jnp.zeros_like(ref)
    slots[0] = run[...]
    greet(sizes, here, bits)
    along_x = Sides(0, sizes, here, fold.at[0], fold.at[nx - 1], xin, sent, came)
    along_x.start()
    tree = Tree(bits, first, here, slots, inbox, tree_sent, tree_came)
    tree.start(0)
    acc[...] = fold[1 : nx - 1]
    along_x.arrive()
    acc[0] += xin[0]
    acc[cx - 1] += xin[1]
    for x in range(cx):
        yout[0, x : x + 1, :] = acc[x, 0:1, :]
        yout[1, x : x + 1, :] = acc[x, cy + 1 : cy + 2, :]
    along_y = Sides(1, sizes, here, yout.at[0], yout.at[1], yin, sent, came)
    along_y.start()
    tree.step(0)
    tree.start(1)
    along_y.arrive()
    for x in range(cx):
        acc[x, 1:2, :] += yin[0, x : x + 1, :]
        acc[x, cy : cy + 1, :] += yin[1, x : x + 1, :]
    turned = acc[:, :, size : size + 128].reshape(cx * tall, 128).T
    zout[...] = turned[0:8]
    along_z = Sides(2, sizes, here, zout, zout, zin, sent, came)
    along_z.start()
    for n in range(1, len(bits)):
        tree.step(n)
        tree.start(n + 1)
    last = slots[len(bits)]
    answer = base[:, 0:1]
    for l in range(sep.shape[0]):
        answer = answer + jnp.sum(sep[l] * last[l : l + 1], axis=1, keepdims=True)
    unknowns = answer.shape[0]
    inside = lax.broadcasted_iota(jnp.int32, (unknowns, size), 1) // (2 * PTS) == lax.broadcasted_iota(
        jnp.int32, (unknowns, size), 0
    )
    line = jnp.sum(jnp.where(inside, answer, 0.0), axis=0, keepdims=True)
    for x in range(cx):
        bump = basis[x % PTS] * line
        for y in range(0, cy, PTS):
            out[x, y : y + PTS, :] = acc[x, y + 1 : y + 1 + PTS, 0:size] + bump
    along_z.arrive()
    padded = cx * tall
    row = lax.broadcasted_iota(jnp.int32, (8, padded), 0)
    low = jnp.where(row == 0, zin[0, 1:2, :], 0.0)
    high = jnp.where(row == 7, zin[1, 0:1, :], 0.0)
    turned = jnp.concatenate([low, jnp.zeros((112, padded), F32), high], 0).T.reshape(cx, tall, 128)
    lane = lax.broadcasted_iota(jnp.int32, (1, 128), 1)
    extra = turned[:, 1 : cy + 1]
    out[:, :, 0:128] += jnp.where(lane < 64, extra, 0.0)
    out[:, :, size - 128 : size] += jnp.where(lane >= 64, extra, 0.0)
    for sides in (along_x, along_y, along_z):
        sides.finish()
    tree.finish()


def on_device(residual, fdm_vectors, fdm_eigen, coarse_basis, x_interior, x_separator):
    cx, cy, cz = residual.shape
    ex, ey, ez = cx // PTS, cy // PTS, cz // PTS
    sizes = [lax.axis_size(axis) for axis in AXES]
    vectors = fdm_vectors.reshape(fdm_vectors.shape[3:])
    eigen = fdm_eigen.reshape(fdm_eigen.shape[3:])
    own = x_interior.reshape(x_interior.shape[3:])
    sep = x_separator.reshape(x_separator.shape[3:])
    levels, unknowns, width = sep.shape
    basis = jnp.tile(coarse_basis, (1, 1, ez))
    bits = tree_bits(sizes)
    early = bits[:3]
    late = bits[3:]
    nx, tall = cx + 2, PTS * (ey - 1) + ROWS
    deep = -(-levels // 8) * 8
    wide = -(-(nx * tall) // 128) * 128
    flat = -(-nx // 8) * 8
    vmem = pl.BlockSpec(memory_space=pltpu.VMEM)
    dma = pltpu.SemaphoreType.DMA

    def tree_scratch(rounds):
        return [pltpu.VMEM((rounds + 1, deep, width), F32), pltpu.VMEM((max(rounds, 1), deep, width), F32)]

    def semaphores(rounds):
        return [dma((6,)), dma((6,)), dma((max(rounds, 1),)), dma((max(rounds, 1),))]

    grid, ends, run, base = pl.pallas_call(
        functools.partial(halo_kernel, sizes, early),
        out_shape=(
            jax.ShapeDtypeStruct((nx, tall, cz), F32),
            jax.ShapeDtypeStruct((nx, tall, 128), F32),
            jax.ShapeDtypeStruct((deep, width), F32),
            jax.ShapeDtypeStruct((unknowns, 128), F32),
        ),
        in_specs=[vmem] * 4,
        out_specs=(vmem,) * 4,
        scratch_shapes=[
            pltpu.VMEM((2, cy, cz), F32),
            pltpu.VMEM((2, flat, cz), F32),
            pltpu.VMEM((2, flat, cz), F32),
            pltpu.VMEM((2, 8, wide), F32),
            pltpu.VMEM((2, 8, wide), F32),
        ] + tree_scratch(len(early)) + semaphores(len(early)),
        compiler_params=pltpu.CompilerParams(
            collective_id=0, has_side_effects=True, vmem_limit_bytes=32 * 1024 * 1024
        ),
        name="halo",
    )(residual, basis, own, sep)
    folded = smooth_call(grid, ends, vectors, eigen, ex, ey, ez)
    return pl.pallas_call(
        functools.partial(fold_kernel, sizes, late, len(early)),
        out_shape=jax.ShapeDtypeStruct((cx, cy, cz), F32),
        in_specs=[vmem] * 5,
        out_specs=vmem,
        scratch_shapes=[
            pltpu.VMEM((cx, tall, cz + 128), F32),
            pltpu.VMEM((2, tall, cz + 128), F32),
            pltpu.VMEM((2, cx, cz + 128), F32),
            pltpu.VMEM((2, cx, cz + 128), F32),
            pltpu.VMEM((8, cx * tall), F32),
            pltpu.VMEM((2, 8, cx * tall), F32),
        ] + tree_scratch(len(late)) + semaphores(len(late)),
        compiler_params=pltpu.CompilerParams(
            collective_id=1, has_side_effects=True, vmem_limit_bytes=32 * 1024 * 1024
        ),
        name="fold",
    )(folded, basis, sep, run, base)


def solution(mesh):
    in_specs = (
        P("gx", "gy", "gz"),
        P("gx", "gy", "gz", None, None, None, None),
        P("gx", "gy", "gz", None, None, None),
        P(),
        P("gx", "gy", "gz", None, None),
        P("gx", "gy", "gz", None, None, None),
    )
    out_specs = P("gx", "gy", "gz")
    return jax.shard_map(
        on_device, mesh=mesh, in_specs=in_specs, out_specs=out_specs, check_vma=False
    )
```

```python
import functools

import jax
import jax.numpy as jnp
from jax import lax
from jax.experimental import pallas as pl
from jax.experimental.pallas import tpu as pltpu
from jax.sharding import PartitionSpec as P

PTS = 8
EXT = PTS + 2
ROWS = 16
F32 = jnp.float32
BF16 = jnp.bfloat16


def fill_selection(sel, first, last, groups, count):
    lanes = groups * count
    size = count * PTS
    column = lax.broadcasted_iota(jnp.int32, (1, EXT * lanes), 1)
    element = column % lanes
    g, r = element // count, element % count
    z = PTS * r + column // lanes - 1
    target = g * size + z
    target = jnp.where(z < 0, groups * size + 2 * g, target)
    target = jnp.where(z >= size, groups * size + 2 * g + 1, target)
    target = jnp.broadcast_to(target, (ROWS, EXT * lanes))
    row = lax.broadcasted_iota(jnp.int32, (ROWS, EXT * lanes), 0)

    def body(n, _):
        start = pl.multiple_of(n * ROWS, ROWS)
        sel[pl.ds(start, ROWS), :] = jnp.where(row + start == target, 1.0, 0.0).astype(BF16)
        return 0

    lax.fori_loop(first // ROWS, last // ROWS, body, 0)


def halves(value):
    high = value.astype(BF16)
    return high, (value - high.astype(F32)).astype(BF16)


def prepare_modes(vec_ref, eig_ref, modes, lam, lamx):
    def spread(n, _):
        d, i = n // EXT, n % EXT
        rows = vec_ref[d, i].astype(F32)
        for a in range(EXT):
            modes[pl.ds(pl.multiple_of((n * EXT + a) * 8, 8), 8), :] = jnp.broadcast_to(rows[a : a + 1], (8, 128))
        return 0

    lax.fori_loop(0, 3 * EXT, spread, 0)
    for d in range(2):
        rows = eig_ref[d + 1]
        for a in range(EXT):
            lam[(d * EXT + a) * 8 : (d * EXT + a + 1) * 8, :] = jnp.broadcast_to(rows[a : a + 1], (8, 128))
    lamx[...] = jnp.ones_like(lamx)
    lamx[0:EXT, :] = eig_ref[0]


def gather_elements(grid_ref, ends_ref, sel_ref, parts, buf, ex, ey):
    groups = ex * ey
    size = grid_ref.shape[2]
    rows = EXT * ROWS
    ends = None
    for g in range(groups):
        x, y = PTS * (g // ey), PTS * (g % ey)
        block = grid_ref[x : x + EXT, y : y + ROWS, :].reshape(rows, size)
        high, low = halves(block)
        parts[0:rows, g * size : (g + 1) * size] = high
        parts[rows : 2 * rows, g * size : (g + 1) * size] = low
        side = ends_ref[x : x + EXT, y : y + ROWS, :].reshape(rows, 128)
        side = side if g == 0 else pltpu.roll(side, 2 * g, 1)
        ends = side if ends is None else ends + side
    high, low = halves(ends)
    width = groups * size
    parts[0:rows, width : width + 128] = high
    parts[rows : 2 * rows, width : width + 128] = low
    for pair in range(EXT // 2):
        columns = slice(pair * 256, (pair + 1) * 256)
        both = jnp.dot(parts[:, 0:width], sel_ref[0:width, columns], preferred_element_type=F32)
        if pair in (0, EXT // 2 - 1):
            both = both + jnp.dot(
                parts[:, width : width + 128], sel_ref[width : width + 128, columns], preferred_element_type=F32
            )
        total = both[0:rows] + both[rows : 2 * rows]
        buf[2 * pair * rows : (2 * pair + 1) * rows, :] = total[:, 0:128]
        buf[(2 * pair + 1) * rows : (2 * pair + 2) * rows, :] = total[:, 128:256]


def contract(values, modes, d, back):
    out = []
    for p in range(EXT):
        total = None
        for q in range(EXT):
            i, a = (p, q) if back else (q, p)
            start = ((d * EXT + i) * EXT + a) * 8
            term = modes[start : start + 8, :][None] * values[q]
            total = term if total is None else total + term
        out.append(total)
    return out


def tile(ref, start):
    return ref[pl.ds(start, ROWS), :].reshape(2, 8, 128)


def put(ref, start, value):
    ref[pl.ds(start, ROWS), :] = value.reshape(ROWS, 128)


def along_z(buf, modes, back):
    def body(i, _):
        at = [pl.multiple_of((k * EXT + i) * ROWS, ROWS) for k in range(EXT)]
        out = contract([tile(buf, s) for s in at], modes, 2, back)
        for s, value in zip(at, out):
            put(buf, s, value)
        return 0

    lax.fori_loop(0, EXT, body, 0)


def along_xy(buf, turn, modes, lam, lamx):
    def body(c, _):
        at = [pl.multiple_of((c * EXT + i) * ROWS, ROWS) for i in range(EXT)]
        t = contract([tile(buf, s) for s in at], modes, 0, False)
        for a in range(EXT):
            turn[a * ROWS : (a + 1) * ROWS, :] = t[a].reshape(ROWS, 128)
        t = [turn[pl.ds(j, ROWS, ROWS), :].reshape(2, 8, 128) for j in range(EXT)]
        t = contract(t, modes, 1, False)
        first = lamx[...].reshape(2, 8, 128)
        third = lam[pl.ds(pl.multiple_of((EXT + c) * 8, 8), 8), :][None]
        t = [v / (first + lam[b * 8 : (b + 1) * 8, :][None] + third) for b, v in enumerate(t)]
        t = contract(t, modes, 1, True)
        for j in range(EXT):
            turn[j * ROWS : (j + 1) * ROWS, :] = t[j].reshape(ROWS, 128)
        t = [turn[pl.ds(a, ROWS, ROWS), :].reshape(2, 8, 128) for a in range(EXT)]
        t = contract(t, modes, 0, True)
        for s, value in zip(at, t):
            put(buf, s, value)
        return 0

    lax.fori_loop(0, EXT, body, 0)


def scatter_elements(buf, sel_ref, parts, grid_ref, ends_ref, ex, ey):
    groups = ex * ey
    size = grid_ref.shape[2]
    rows = EXT * ROWS
    lanes = EXT * 128
    for k in range(EXT):
        high, low = halves(buf[k * rows : (k + 1) * rows, :])
        parts[0:rows, k * 128 : (k + 1) * 128] = high
        parts[rows : 2 * rows, k * 128 : (k + 1) * 128] = low
    dims = (((1,), (1,)), ((), ()))
    grid_ref[...] = jnp.zeros_like(grid_ref)
    ends_ref[...] = jnp.zeros_like(ends_ref)
    width = groups * size
    both = lax.dot_general(
        parts[:, 0:lanes], sel_ref[width : width + 128, :], dims, preferred_element_type=F32
    )
    ends = both[0:rows] + both[rows : 2 * rows]
    lane = lax.broadcasted_iota(jnp.int32, (1, 128), 1)
    for g in range(groups):
        x, y = PTS * (g // ey), PTS * (g % ey)
        both = lax.dot_general(
            parts[:, 0:lanes], sel_ref[g * size : (g + 1) * size, :], dims, preferred_element_type=F32
        )
        total = (both[0:rows] + both[rows : 2 * rows]).reshape(EXT, ROWS, size)
        grid_ref[x : x + EXT, y : y + EXT, :] += total[:, 0:EXT]
        side = ends if g == 0 else pltpu.roll(ends, 128 - 2 * g, 1)
        side = jnp.where(lane < 2, side, 0.0).reshape(EXT, ROWS, 128)
        ends_ref[x : x + EXT, y : y + EXT, :] += side[:, 0:EXT]


def smooth_kernel(ex, ey, grid_in, ends_in, vec, eig, sel, out, parts, buf, turn, modes, lam, lamx):
    size = grid_in.shape[2]
    grid_out, ends_out = out.at[:, :, 0:size], out.at[:, :, size : size + 128]
    turn[...] = jnp.zeros_like(turn)
    prepare_modes(vec, eig, modes, lam, lamx)
    gather_elements(grid_in, ends_in, sel, parts, buf, ex, ey)
    along_z(buf, modes, False)
    along_xy(buf, turn, modes, lam, lamx)
    along_z(buf, modes, True)
    scatter_elements(buf, sel, parts, grid_out, ends_out, ex, ey)


def smooth_call(grid, ends, vectors, eigen, sel, ex, ey):
    nx, tall, size = grid.shape
    vmem = pl.BlockSpec(memory_space=pltpu.VMEM)
    rows = EXT * ROWS
    return pl.pallas_call(
        functools.partial(smooth_kernel, ex, ey),
        out_shape=jax.ShapeDtypeStruct((nx, tall, size + 128), F32),
        in_specs=[vmem] * 5,
        out_specs=vmem,
        scratch_shapes=[
            pltpu.VMEM((2 * rows, max(sel.shape)), BF16),
            pltpu.VMEM((EXT * rows, 128), F32),
            pltpu.VMEM((ROWS * ROWS, 128), F32),
            pltpu.VMEM((3 * EXT * EXT * 8, 128), F32),
            pltpu.VMEM((2 * EXT * 8, 128), F32),
            pltpu.VMEM((ROWS, 128), F32),
        ],
        compiler_params=pltpu.CompilerParams(vmem_limit_bytes=20 * 1024 * 1024),
        name="smooth",
    )(grid, ends, vectors, eigen, sel)


AXES = ("gx", "gy", "gz")
MESH = pl.DeviceIdType.MESH


def tree_bits(sizes):
    return [(a, 1 << b) for a in (2, 1, 0) for b in range(sizes[a].bit_length() - 1)]


def greet(sizes, here, bits):
    barrier = pltpu.get_barrier_semaphore()
    for a in range(3):
        for step in (-1, 1):
            @pl.when((here[a] + step >= 0) & (here[a] + step < sizes[a]))
            def _(a=a, step=step):
                pl.semaphore_signal(barrier, inc=1, device_id={AXES[a]: here[a] + step}, device_id_type=MESH)
    for a, bit in bits:
        pl.semaphore_signal(barrier, inc=1, device_id={AXES[a]: partner(here[a], bit)}, device_id_type=MESH)
    peers = len(bits)
    for a in range(3):
        peers = peers + jnp.where(here[a] > 0, 1, 0) + jnp.where(here[a] < sizes[a] - 1, 1, 0)
    pl.semaphore_wait(barrier, peers)


def partner(index, bit):
    return index + bit * (1 - 2 * ((index // bit) % 2))


class Sides:
    def __init__(self, a, sizes, here, low, high, slots, sent, came):
        self.below, self.above = here[a] > 0, here[a] < sizes[a] - 1
        self.down = pltpu.make_async_remote_copy(
            low, slots.at[1], sent.at[2 * a], came.at[2 * a + 1],
            device_id={AXES[a]: here[a] - 1}, device_id_type=MESH,
        )
        self.up = pltpu.make_async_remote_copy(
            high, slots.at[0], sent.at[2 * a + 1], came.at[2 * a],
            device_id={AXES[a]: here[a] + 1}, device_id_type=MESH,
        )

    def start(self):
        pl.when(self.below)(self.down.start)
        pl.when(self.above)(self.up.start)

    def arrive(self):
        pl.when(self.below)(self.up.wait_recv)
        pl.when(self.above)(self.down.wait_recv)

    def finish(self):
        pl.when(self.below)(self.down.wait_send)
        pl.when(self.above)(self.up.wait_send)


class Tree:
    def __init__(self, bits, first, here, slots, inbox, sent, came):
        self.first, self.slots, self.inbox = first, slots, inbox
        self.copies = [
            pltpu.make_async_remote_copy(
                slots.at[n], inbox.at[n], sent.at[n], came.at[n],
                device_id={AXES[a]: partner(here[a], bit)}, device_id_type=MESH,
            )
            for n, (a, bit) in enumerate(bits)
        ]

    def start(self, n):
        if n < len(self.copies):
            self.copies[n].start()

    def step(self, n):
        if n < len(self.copies):
            self.copies[n].wait_recv()
            level = lax.broadcasted_iota(jnp.int32, self.slots.shape[1:], 0)
            self.slots[n + 1] = self.slots[n] + jnp.where(level >= self.first + n, self.inbox[n], 0.0)

    def finish(self):
        for copy in self.copies:
            copy.wait_send()


def place():
    return [lax.axis_index(axis) for axis in AXES]


def halo_kernel(sizes, bits, res_far, basis_in, own_far, sep_far, grid, ends, run, base, basis, sel, res, own, sep, loaded, xin, yout, yin, zout, zin, slots, inbox,
                sent, came, tree_sent, tree_came):
    cx, cy, size = res.shape
    nx, tall = cx + 2, grid.shape[1]
    here = place()
    loads = [
        pltpu.make_async_copy(far, near, loaded.at[n])
        for n, (far, near) in enumerate(((res_far, res), (own_far, own), (sep_far, sep)))
    ]
    for load in loads:
        load.start()
    for ref in (xin, yin, zin, grid, slots, yout):
        ref[...] = jnp.zeros_like(ref)
    repeat = lax.broadcasted_iota(jnp.int32, (PTS, size), 1) % PTS == lax.broadcasted_iota(jnp.int32, (PTS, size), 0)
    basis[...] = jnp.dot(
        basis_in[...].reshape(PTS * PTS, PTS),
        jnp.where(repeat, 1.0, 0.0),
        precision=lax.Precision.HIGHEST,
        preferred_element_type=F32,
    ).reshape(basis.shape)
    greet(sizes, here, bits)
    for load in loads:
        load.wait()
    along_x = Sides(0, sizes, here, res.at[0], res.at[cx - 1], xin, sent, came)
    along_x.start()

    span = 2 * PTS
    weighted = jnp.zeros((PTS, size), F32)
    for x in range(cx):
        for y in range(0, cy, PTS):
            weighted = weighted + res[x, y : y + PTS, :] * basis[x % PTS]
    unknowns = own.shape[0]
    line = jnp.sum(weighted, axis=0, keepdims=True)
    inside = lax.broadcasted_iota(jnp.int32, (unknowns, size), 1) // span == lax.broadcasted_iota(
        jnp.int32, (unknowns, size), 0
    )
    rhs = jnp.sum(jnp.where(inside, line, 0.0), axis=1, keepdims=True)
    for l in range(sep.shape[0]):
        slots[0, l : l + 1, :] = jnp.sum(sep[l] * rhs, axis=0, keepdims=True)
    tree = Tree(bits, 0, here, slots, inbox, tree_sent, tree_came)
    tree.start(0)
    coef = jnp.sum(own[...] * rhs, axis=0, keepdims=True)
    base[...] = jnp.broadcast_to(jnp.sum(own[...] * coef, axis=1, keepdims=True), base.shape)
    for x in range(cx):
        grid[x + 1, 1 : cy + 1, :] = res[x]

    groups = (cx // PTS) * (cy // PTS)
    cuts = [ROWS * (n * sel.shape[0] // (3 * ROWS)) for n in range(4)]
    fill_selection(sel, cuts[0], cuts[1], groups, size // PTS)
    along_x.arrive()
    grid[0, 1 : cy + 1, :] = xin[0]
    grid[nx - 1, 1 : cy + 1, :] = xin[1]
    for x in range(nx):
        yout[0, x : x + 1, :] = grid[x, 1:2, :]
        yout[1, x : x + 1, :] = grid[x, cy : cy + 1, :]
    along_y = Sides(1, sizes, here, yout.at[0], yout.at[1], yin, sent, came)
    along_y.start()
    tree.step(0)
    tree.start(1)
    fill_selection(sel, cuts[1], cuts[2], groups, size // PTS)
    along_y.arrive()
    for x in range(nx):
        grid[x, 0:1, :] = yin[0, x : x + 1, :]
        grid[x, cy + 1 : cy + 2, :] = yin[1, x : x + 1, :]

    lane = lax.broadcasted_iota(jnp.int32, (1, 128), 1)
    rows = nx * tall
    padded = zout.shape[2]
    flat = grid[...].reshape(rows, size)
    both = jnp.where(lane == 0, flat[:, 0:128], flat[:, size - 128 : size])
    both = jnp.concatenate([both, jnp.zeros((padded - rows, 128), F32)], 0)
    turned = both.T
    zout[0] = turned[0:8]
    zout[1] = turned[120:128]
    along_z = Sides(2, sizes, here, zout.at[0], zout.at[1], zin, sent, came)
    along_z.start()
    tree.step(1)
    tree.start(2)
    fill_selection(sel, cuts[2], cuts[3], groups, size // PTS)
    along_z.arrive()
    row = lax.broadcasted_iota(jnp.int32, (8, padded), 0)
    head = jnp.where(row == 0, zin[0, 7:8, :], jnp.where(row == 1, zin[1, 0:1, :], 0.0))
    turned = jnp.concatenate([head, jnp.zeros((120, padded), F32)], 0).T
    ends[...] = turned[0:rows].reshape(nx, tall, 128)
    for n in range(2, len(bits)):
        tree.step(n)
        tree.start(n + 1)
    run[...] = slots[len(bits)]
    for sides in (along_x, along_y, along_z):
        sides.finish()
    tree.finish()


def fold_kernel(sizes, bits, first, fold, basis, sep, run, base, out, acc, xin, yout, yin, zout, zin, slots, inbox,
                sent, came, tree_sent, tree_came):
    cx, cy, size = out.shape
    nx, tall = cx + 2, fold.shape[1]
    here = place()
    for ref in (xin, yin, zin):
        ref[...] = jnp.zeros_like(ref)
    slots[0] = run[...]
    greet(sizes, here, bits)
    along_x = Sides(0, sizes, here, fold.at[0], fold.at[nx - 1], xin, sent, came)
    along_x.start()
    tree = Tree(bits, first, here, slots, inbox, tree_sent, tree_came)
    tree.start(0)
    acc[...] = fold[1 : nx - 1]
    along_x.arrive()
    acc[0] += xin[0]
    acc[cx - 1] += xin[1]
    for x in range(cx):
        yout[0, x : x + 1, :] = acc[x, 0:1, :]
        yout[1, x : x + 1, :] = acc[x, cy + 1 : cy + 2, :]
    along_y = Sides(1, sizes, here, yout.at[0], yout.at[1], yin, sent, came)
    along_y.start()
    tree.step(0)
    tree.start(1)
    along_y.arrive()
    for x in range(cx):
        acc[x, 1:2, :] += yin[0, x : x + 1, :]
        acc[x, cy : cy + 1, :] += yin[1, x : x + 1, :]
    turned = acc[:, :, size : size + 128].reshape(cx * tall, 128).T
    zout[...] = turned[0:8]
    along_z = Sides(2, sizes, here, zout, zout, zin, sent, came)
    along_z.start()
    for n in range(1, len(bits)):
        tree.step(n)
        tree.start(n + 1)
    last = slots[len(bits)]
    answer = base[:, 0:1]
    for l in range(sep.shape[0]):
        answer = answer + jnp.sum(sep[l] * last[l : l + 1], axis=1, keepdims=True)
    unknowns = answer.shape[0]
    inside = lax.broadcasted_iota(jnp.int32, (unknowns, size), 1) // (2 * PTS) == lax.broadcasted_iota(
        jnp.int32, (unknowns, size), 0
    )
    line = jnp.sum(jnp.where(inside, answer, 0.0), axis=0, keepdims=True)
    for x in range(cx):
        bump = basis[x % PTS] * line
        for y in range(0, cy, PTS):
            out[x, y : y + PTS, :] = acc[x, y + 1 : y + 1 + PTS, 0:size] + bump
    along_z.arrive()
    padded = cx * tall
    row = lax.broadcasted_iota(jnp.int32, (8, padded), 0)
    low = jnp.where(row == 0, zin[0, 1:2, :], 0.0)
    high = jnp.where(row == 7, zin[1, 0:1, :], 0.0)
    turned = jnp.concatenate([low, jnp.zeros((112, padded), F32), high], 0).T.reshape(cx, tall, 128)
    lane = lax.broadcasted_iota(jnp.int32, (1, 128), 1)
    extra = turned[:, 1 : cy + 1]
    out[:, :, 0:128] += jnp.where(lane < 64, extra, 0.0)
    out[:, :, size - 128 : size] += jnp.where(lane >= 64, extra, 0.0)
    for sides in (along_x, along_y, along_z):
        sides.finish()
    tree.finish()


def on_device(residual, fdm_vectors, fdm_eigen, coarse_basis, x_interior, x_separator):
    cx, cy, cz = residual.shape
    ex, ey, ez = cx // PTS, cy // PTS, cz // PTS
    sizes = [lax.axis_size(axis) for axis in AXES]
    vectors = fdm_vectors.reshape(fdm_vectors.shape[3:])
    eigen = fdm_eigen.reshape(fdm_eigen.shape[3:])
    own = x_interior.reshape(x_interior.shape[3:])
    sep = x_separator.reshape(x_separator.shape[3:])
    levels, unknowns, width = sep.shape
    bits = tree_bits(sizes)
    early = bits[:3]
    late = bits[3:]
    nx, tall = cx + 2, PTS * (ey - 1) + ROWS
    deep = -(-levels // 8) * 8
    wide = -(-(nx * tall) // 128) * 128
    flat = -(-nx // 8) * 8
    vmem = pl.BlockSpec(memory_space=pltpu.VMEM)
    far = pl.BlockSpec(memory_space=pltpu.HBM)
    dma = pltpu.SemaphoreType.DMA

    def tree_scratch(rounds):
        return [pltpu.VMEM((rounds + 1, deep, width), F32), pltpu.VMEM((max(rounds, 1), deep, width), F32)]

    def semaphores(rounds):
        return [dma((6,)), dma((6,)), dma((max(rounds, 1),)), dma((max(rounds, 1),))]

    grid, ends, run, base, basis, sel = pl.pallas_call(
        functools.partial(halo_kernel, sizes, early),
        out_shape=(
            jax.ShapeDtypeStruct((nx, tall, cz), F32),
            jax.ShapeDtypeStruct((nx, tall, 128), F32),
            jax.ShapeDtypeStruct((deep, width), F32),
            jax.ShapeDtypeStruct((unknowns, 128), F32),
            jax.ShapeDtypeStruct((PTS, PTS, cz), F32),
            jax.ShapeDtypeStruct((ex * ey * cz + 128, EXT * ex * ey * ez), BF16),
        ),
        in_specs=[far, vmem, far, far],
        out_specs=(vmem,) * 6,
        scratch_shapes=[
            pltpu.VMEM((cx, cy, cz), F32),
            pltpu.VMEM(own.shape, F32),
            pltpu.VMEM(sep.shape, F32),
            dma((3,)),
            pltpu.VMEM((2, cy, cz), F32),
            pltpu.VMEM((2, flat, cz), F32),
            pltpu.VMEM((2, flat, cz), F32),
            pltpu.VMEM((2, 8, wide), F32),
            pltpu.VMEM((2, 8, wide), F32),
        ] + tree_scratch(len(early)) + semaphores(len(early)),
        compiler_params=pltpu.CompilerParams(
            collective_id=0, has_side_effects=True, vmem_limit_bytes=12 * 1024 * 1024
        ),
        name="halo",
    )(residual, coarse_basis, own, sep)
    folded = smooth_call(grid, ends, vectors, eigen, sel, ex, ey)
    return pl.pallas_call(
        functools.partial(fold_kernel, sizes, late, len(early)),
        out_shape=jax.ShapeDtypeStruct((cx, cy, cz), F32),
        in_specs=[vmem] * 5,
        out_specs=vmem,
        scratch_shapes=[
            pltpu.VMEM((cx, tall, cz + 128), F32),
            pltpu.VMEM((2, tall, cz + 128), F32),
            pltpu.VMEM((2, cx, cz + 128), F32),
            pltpu.VMEM((2, cx, cz + 128), F32),
            pltpu.VMEM((8, cx * tall), F32),
            pltpu.VMEM((2, 8, cx * tall), F32),
        ] + tree_scratch(len(late)) + semaphores(len(late)),
        compiler_params=pltpu.CompilerParams(
            collective_id=1, has_side_effects=True, vmem_limit_bytes=12 * 1024 * 1024
        ),
        name="fold",
    )(folded, basis, sep, run, base)


def solution(mesh):
    in_specs = (
        P("gx", "gy", "gz"),
        P("gx", "gy", "gz", None, None, None, None),
        P("gx", "gy", "gz", None, None, None),
        P(),
        P("gx", "gy", "gz", None, None),
        P("gx", "gy", "gz", None, None, None),
    )
    out_specs = P("gx", "gy", "gz")
    return jax.shard_map(
        on_device, mesh=mesh, in_specs=in_specs, out_specs=out_specs, check_vma=False
    )
```
